32 devices in a mesh: die: 2 (over y), row: 4 (over z), col: 4 (over x, core).
Axes of the slice: x: 2, y: 2, z: 4, core: 2. Of those that a mesh axis runs over, the one named last changes fastest.
Arguments:
- parcel_patch: float32 [4, 2048, 256], P('die', ('row', 'col')), may hold values from 0.1 to 1
- target_unit: int32 [4, 2048, 1], P('die', ('row', 'col')), may hold values from 0 to 15; in each aligned block of 128 rows (0 to 127, 128 to 255, ..., all dimensions but the last counted through in order) at most 16 rows name the same one
- target_patch: int32 [4, 2048], P('die', ('row', 'col')), may hold values from 0 to 127
- across_taps: float32 [8, 255], replicated, may hold values from -0.375 to 0.375
- down_taps: float32 [8, 255], replicated, may hold values from -0.375 to 0.375
- source_heated_mixing: float32 [8, 4, 4], replicated, may hold values from -2.4 to 2.4
Outputs:
- chip_heat_increase: float32 [4, 512, 1024], P('die', 'row', 'col')
- block_power_slopes: float32 [4, 2048, 256], P('die', ('row', 'col'))
The draws below stay inside these ranges and needn't reach their ends.
Inputs may be any that keep to these rules, and one draw needn't show every extreme that they name: `target_unit`: among the 128 blocks of one die held by one device (aligned blocks of rows), at most 16 name the same device, and in every draw some such group names one device exactly 16 times.
All inputs are finite; a program needn't handle non-finite values.
Results may differ from the reference program's by a relative error of at most 0.0002.
Values sent between devices are 32-bit elements; how exact they have to be, the bound alone decides.
A program may use at most 192 MiB of HBM per device.

```python
import math
import jax
import jax.numpy as jnp
import numpy as np
from jax import lax

STACK_CHIPS = 4
KERNEL_MODES = 8
TAPS = 255
PATCH_SIDE = 16
UNIT_MESH_X = 128
UNIT_MESH_Y = 256
PARCELS_PER_UNIT = 128
PARCELS = 2048
PARCEL_LIMIT = 16
PATCH_AREA = 256
CELLS_ALONG_ONE = 512
CELLS_ALONG_TWO = 1024
N_ROW = 4
N_COL = 4


def set_ends(array, own_key, least, largest):
    dims = array.shape
    spot = [jax.random.randint(jax.random.fold_in(own_key, axis), (), 0, dims[axis]) for axis in range(len(dims))]
    array = array.at[tuple(spot)].set(least)
    longest = dims.index(max(dims))
    spot[longest] = (spot[longest] + 1) % dims[longest]
    return array.at[tuple(spot)].set(largest)


def shard_levels(stream_key, dims, pieces, smallest, high):
    gain, own = 1.0, jax.random.fold_in(stream_key, 6)
    for position, parts in pieces:
        steps = jnp.exp(jax.random.uniform(jax.random.fold_in(own, position), (parts,), jnp.float32, smallest / len(pieces), high / len(pieces)))
        gain = gain * jnp.repeat(steps, dims[position] // parts).reshape([-1 if axis == position else 1 for axis in range(len(dims))])
    return gain


def routed_block(stream_key, own, number, rows, number_of, top, most, lean):
    sequence = jax.random.permutation(stream_key, number_of)
    packed, usual = shares(number_of, rows * top, most, lean, True), shares(number_of, rows * top, most, lean, False)
    places = jnp.arange(number_of)

    def named(sizes, offset_by):
        used = int((sizes > 0).sum())
        fixed = max(1, used // 4)
        passed = fixed + (places - fixed + offset_by * (used - fixed)) % max(1, number_of - fixed)
        return jnp.zeros((number_of,), jnp.int32).at[sequence[jnp.where(places < fixed, places, passed)]].set(jnp.asarray(sizes, jnp.int32))

    sizes = jnp.where(number % 4 == 0, named(packed, number // 4), named(usual, number - number // 4 - 1))
    mixed = jax.random.permutation(jax.random.fold_in(own, 3), number_of)
    donor, taker = mixed[0:number_of // 2 * 2:2], mixed[1:number_of // 2 * 2:2]
    room = jnp.minimum(sizes[donor] - 1, most - sizes[taker]) // 2
    room = jnp.where((donor == sequence[0]) | (taker == sequence[0]) | (sizes[taker] == 0), 0, jnp.maximum(room, 0))
    passed = jax.random.randint(jax.random.fold_in(own, 4), (number_of // 2,), 0, 1 << 20) % (room + 1)
    sizes = sizes.at[donor].add(-passed).at[taker].add(passed)
    items = jnp.searchsorted(jnp.cumsum(sizes), jnp.arange(rows * top), side="right").astype(jnp.int32)
    table = items.reshape(top, rows).T
    table = table[jax.random.permutation(jax.random.fold_in(own, 1), rows)]
    offset_by = jax.random.randint(jax.random.fold_in(own, 2), (rows, 1), 0, top)
    return jnp.take_along_axis(table, (jnp.arange(top)[None, :] + offset_by) % top, axis=1)


def shares(count, total, reach, lean, full):
    portions = [(1 << 20) // math.isqrt(standing ** lean) + 1 for standing in range(1, count + 1)]
    largest = reach if full else min(reach, max(-(-total // count), total * portions[0] // sum(portions)))
    least = 1 if total - largest >= count - 1 else 0
    holding, surplus = [largest] + [least] * (count - 1), total - largest - least * (count - 1)
    while surplus > 0:
        candidates = [i for i in range(1, count) if holding[i] < largest] or [i for i in range(1, count) if holding[i] < reach]
        whole, left = sum([portions[i] for i in candidates]), surplus
        for i in candidates:
            addition = min(reach - holding[i], max(1, left * portions[i] // whole), surplus)
            holding[i] = holding[i] + addition
            surplus = surplus - addition
    return np.array(holding)


def centred(rng, shape, scale, bound, kind=jnp.bfloat16):
    values = scale * jax.random.normal(rng, shape, jnp.float32)
    return jnp.clip(values, min=-bound, max=bound).astype(kind)


def setup_inputs(seed: int = 0) -> dict:
    key_of = jax.random.split(jax.random.key(seed), 7)
    parcel_patch = jnp.clip(jnp.exp(math.log(1.0) - 2.3025851 * jax.random.uniform(key_of[0], (STACK_CHIPS, PARCELS, PATCH_AREA), jnp.float32) ** shard_levels(key_of[0], (STACK_CHIPS, PARCELS, PATCH_AREA), ((0, 2), (1, 16)), -0.2, 0.2)), 0.1, 1.0)
    target_unit_keys = jax.random.split(jax.random.fold_in(key_of[1], 1), STACK_CHIPS * PARCELS // PARCELS_PER_UNIT)
    target_unit_turns = jax.random.permutation(jax.random.fold_in(key_of[1], 3), STACK_CHIPS * PARCELS // PARCELS_PER_UNIT)
    target_unit = jax.vmap(lambda own, number: routed_block(jax.random.fold_in(key_of[1], 2), own, number, PARCELS_PER_UNIT, N_ROW * N_COL, 1, PARCEL_LIMIT, 2))(target_unit_keys, target_unit_turns).reshape((STACK_CHIPS, PARCELS, 1))
    target_patch = set_ends(jax.random.randint(key_of[2], (STACK_CHIPS, PARCELS), 0, PARCELS_PER_UNIT), jax.random.fold_in(key_of[2], 1), 0, PARCELS_PER_UNIT - 1).astype(jnp.int32)
    across_taps = centred(key_of[3], (KERNEL_MODES, TAPS), TAPS ** -0.5, 0.375, jnp.float32)
    down_taps = centred(key_of[4], (KERNEL_MODES, TAPS), TAPS ** -0.5, 0.375, jnp.float32)
    source_heated_mixing = centred(key_of[5], (KERNEL_MODES, STACK_CHIPS, STACK_CHIPS), 0.4, 2.4, jnp.float32)
    return dict(parcel_patch=parcel_patch, target_unit=target_unit, target_patch=target_patch, across_taps=across_taps, down_taps=down_taps, source_heated_mixing=source_heated_mixing)


def correlate(source, kernel_taps, along):
    moved_axis = jnp.moveaxis(source, along, -1)
    length = moved_axis.shape[-1]
    tap_count = kernel_taps.shape[0]
    margin = (tap_count - 1) // 2
    extent = length + tap_count - 1
    spectrum = jnp.fft.rfft(moved_axis, extent, axis=-1) * jnp.fft.rfft(kernel_taps[::-1], extent)
    full_corr = jnp.fft.irfft(spectrum, extent, axis=-1)
    return jnp.moveaxis(full_corr[..., margin:margin + length], -1, along)


def reference(parcel_patch, target_unit, target_patch, across_taps, down_taps, source_heated_mixing):
    mesh_amount_name = N_ROW * N_COL
    tile_index = (target_unit[:, :, 0] * PARCELS_PER_UNIT + target_patch).astype(jnp.int32)
    layer_lines = jnp.arange(STACK_CHIPS, dtype=jnp.int32)[:, None]
    patch_totals_acc = jnp.zeros((STACK_CHIPS, mesh_amount_name * PARCELS_PER_UNIT, PATCH_SIDE * PATCH_SIDE), jnp.float32)
    patch_totals_acc = patch_totals_acc.at[layer_lines, tile_index].add(parcel_patch)
    mesh_layout = patch_totals_acc.reshape(STACK_CHIPS, N_ROW, N_COL, UNIT_MESH_X // PATCH_SIDE, UNIT_MESH_Y // PATCH_SIDE, PATCH_SIDE, PATCH_SIDE)
    wattage_field = mesh_layout.transpose(0, 1, 3, 5, 2, 4, 6).reshape(STACK_CHIPS, CELLS_ALONG_ONE, CELLS_ALONG_TWO)
    chip_heat_increase = jnp.zeros((STACK_CHIPS, CELLS_ALONG_ONE, CELLS_ALONG_TWO), jnp.float32)
    for warmth_addend_ordinal in range(KERNEL_MODES):
        warmth_portion = correlate(correlate(wattage_field, across_taps[warmth_addend_ordinal], 1), down_taps[warmth_addend_ordinal], 2)
        chip_heat_increase = chip_heat_increase + jnp.einsum("mu,ung->mng", source_heated_mixing[warmth_addend_ordinal], warmth_portion, precision=lax.Precision.HIGHEST)
    hottest_backward_initial = jax.nn.sigmoid(chip_heat_increase)
    adjoint_field_map = jnp.zeros((STACK_CHIPS, CELLS_ALONG_ONE, CELLS_ALONG_TWO), jnp.float32)
    for warmth_addend_ordinal in range(KERNEL_MODES):
        response = correlate(correlate(hottest_backward_initial, across_taps[warmth_addend_ordinal][::-1], 1), down_taps[warmth_addend_ordinal][::-1], 2)
        adjoint_field_map = adjoint_field_map + jnp.einsum("de,dxy->exy", source_heated_mixing[warmth_addend_ordinal], response, precision=lax.Precision.HIGHEST)
    adjoint_layout = adjoint_field_map.reshape(STACK_CHIPS, N_ROW, UNIT_MESH_X // PATCH_SIDE, PATCH_SIDE, N_COL, UNIT_MESH_Y // PATCH_SIDE, PATCH_SIDE)
    adjoint_patches = adjoint_layout.transpose(0, 1, 4, 2, 5, 3, 6).reshape(STACK_CHIPS, mesh_amount_name * PARCELS_PER_UNIT, PATCH_SIDE * PATCH_SIDE)
    block_power_slopes = adjoint_patches[layer_lines, tile_index]
    return chip_heat_increase, block_power_slopes
```

```python
import jax
import jax.numpy as jnp
from jax import lax
from jax.sharding import PartitionSpec as P

PATCH_SIDE = 16
UNIT_MESH_X = 128
UNIT_MESH_Y = 256


high = lax.Precision.HIGH


def with_halo(cells, sides, width):
    for axis, dim in sides:
        count = lax.axis_size(axis)
        ends = count - 1
        head = lax.slice_in_dim(cells, 0, width, axis=dim)
        tail = lax.slice_in_dim(cells, cells.shape[dim] - width, cells.shape[dim], axis=dim)
        cells = jnp.concatenate(
            [
                lax.ppermute(tail, axis, [(i, (i + 1) % count) for i in range(ends)]),
                cells,
                lax.ppermute(head, axis, [((i + 1) % count, i) for i in range(ends)]),
            ],
            axis=dim,
        )
    return cells


def toeplitz(kernel_taps, length):
    term_count, tap_count = kernel_taps.shape
    extent = length + tap_count - 1
    row = jnp.pad(kernel_taps, ((0, 0), (0, extent + 1 - tap_count)))
    skew = jnp.broadcast_to(row[:, None, :], (term_count, length, extent + 1))
    return skew.reshape(term_count, -1)[:, : length * extent].reshape(term_count, length, extent)


def filtered(fields, across_band, down_band):
    margin = (across_band.shape[2] - across_band.shape[1]) // 2
    padded = with_halo(fields, (("row", 1), ("col", 2)), margin)
    across = jnp.einsum("tab,kbc->takc", across_band, padded, precision=high)
    return jnp.einsum("takc,tyc->taky", across, down_band, precision=high)


def tiles_to_map(patch_totals_acc, tiles_down):
    dies_here, tile_total, cell_count = patch_totals_acc.shape
    mesh_layout = patch_totals_acc.reshape(
        dies_here, tile_total // tiles_down, tiles_down, PATCH_SIDE, PATCH_SIDE
    )
    return mesh_layout.transpose(0, 1, 3, 2, 4).reshape(
        dies_here, tile_total // tiles_down * PATCH_SIDE, tiles_down * PATCH_SIDE
    )


def map_to_tiles(source, tiles_down):
    dies_here, rows_all, cols_all = source.shape
    mesh_layout = source.reshape(
        dies_here, rows_all // PATCH_SIDE, PATCH_SIDE, tiles_down, PATCH_SIDE
    )
    return mesh_layout.transpose(0, 1, 3, 2, 4).reshape(dies_here, -1, PATCH_SIDE * PATCH_SIDE)


def local(parcel_patch, target_unit, target_patch, across_taps, down_taps, source_heated_mixing):
    dies_here, blocks_here, cells_tile = parcel_patch.shape
    devices_grid = lax.axis_size(("row", "col"))
    capacity = max(2, 2 * blocks_here // devices_grid)
    tiles_down = UNIT_MESH_Y // PATCH_SIDE
    destination = target_unit[:, :, 0]
    columns = jnp.arange(devices_grid, dtype=jnp.int32)
    same = destination[:, :, None] == destination[:, None, :]
    lines = jnp.arange(blocks_here, dtype=jnp.int32)
    earlier = lines[None, :] < lines[:, None]
    position = jnp.sum((same & earlier[None]).astype(jnp.int32), axis=2)
    slot_index = destination * capacity + position
    slots = jnp.arange(devices_grid * capacity, dtype=jnp.int32)
    place = (slot_index[:, :, None] == slots).astype(jnp.float32)
    outgoing = jnp.einsum("kbs,kbc->ksc", place, parcel_patch, precision=high)
    labels = jnp.sum(place * (target_patch.astype(jnp.float32) + 1.0)[:, :, None], axis=1) - 1.0
    arrived, arrived_tile = (
        lax.all_to_all(
            outgoing.reshape(dies_here, devices_grid, capacity, cells_tile),
            ("row", "col"),
            split_axis=1,
            concat_axis=1,
            tiled=True,
        ),
        lax.all_to_all(
            labels.reshape(dies_here, devices_grid, capacity),
            ("row", "col"),
            split_axis=1,
            concat_axis=1,
            tiled=True,
        ),
    )
    incoming = arrived.reshape(dies_here, -1, cells_tile)
    target = arrived_tile.reshape(dies_here, -1).astype(jnp.int32)
    chosen = (target[:, :, None] == lines).astype(jnp.float32)
    patch_totals_acc = jnp.einsum("kst,ksc->ktc", chosen, incoming, precision=high)
    wattage_field = tiles_to_map(patch_totals_acc, tiles_down)
    across_band = toeplitz(across_taps, UNIT_MESH_X)
    down_band = toeplitz(down_taps, UNIT_MESH_Y)
    first_die = lax.axis_index("die") * dies_here
    own_columns = lax.dynamic_slice_in_dim(source_heated_mixing, first_die, dies_here, 2)
    heat_terms = filtered(wattage_field, across_band, down_band)
    objective_local_derivative = jnp.einsum(
        "tdk,taky->day", own_columns, heat_terms, precision=high
    )
    chip_heat_increase = lax.psum_scatter(
        objective_local_derivative, "die", scatter_dimension=0, tiled=True
    )
    hottest_backward_initial = jax.nn.sigmoid(chip_heat_increase)
    back_across = toeplitz(across_taps[:, ::-1], UNIT_MESH_X)
    back_down = toeplitz(down_taps[:, ::-1], UNIT_MESH_Y)
    response = filtered(hottest_backward_initial, back_across, back_down)
    own_rows = lax.dynamic_slice_in_dim(source_heated_mixing, first_die, dies_here, 1)
    partial_sens = jnp.einsum("tke,taky->eay", own_rows, response, precision=high)
    adjoint_field_map = lax.psum_scatter(partial_sens, "die", scatter_dimension=0, tiled=True)
    adjoint_patches = map_to_tiles(adjoint_field_map, tiles_down)
    answers = jnp.einsum("kst,ktc->ksc", chosen, adjoint_patches, precision=high)
    returned = lax.all_to_all(
        answers.reshape(dies_here, devices_grid, capacity, cells_tile),
        ("row", "col"),
        split_axis=1,
        concat_axis=1,
        tiled=True,
    )
    block_power_slopes = jnp.einsum(
        "kbs,ksc->kbc", place, returned.reshape(dies_here, -1, cells_tile), precision=high
    )
    return (chip_heat_increase, block_power_slopes)


def solution(mesh):
    placed = (
        P("die", ("row", "col"), None),
        P("die", ("row", "col"), None),
        P("die", ("row", "col")),
        P(),
        P(),
        P(),
    )
    return jax.shard_map(
        local,
        mesh=mesh,
        in_specs=placed,
        out_specs=(P("die", "row", "col"), P("die", ("row", "col"), None)),
        check_vma=False,
    )
```

```python
import functools

import jax
import jax.numpy as jnp
from jax import lax
from jax.experimental import pallas as pl
from jax.experimental.pallas import tpu as pltpu
from jax.sharding import PartitionSpec as P

PATCH_SIDE = 16
UNIT_MESH_X = 128
UNIT_MESH_Y = 256
HALO = 128


high = lax.Precision.HIGH


def two_halves(values):
    head = values.astype(jnp.bfloat16)
    return head, (values - head.astype(jnp.float32)).astype(jnp.bfloat16)


def stage_kernel(
    is_seed, x_ref, across_ref, down_ref, mix_ref, out_ref,
    pad, a_cat, d_cat, p_cat, y_all, acc, got, send, recv,
):
    here, a, b = x_ref.shape
    terms = across_ref.shape[0]
    h = HALO
    row, col, die = lax.axis_index("row"), lax.axis_index("col"), lax.axis_index("die")
    has_up, has_down = row > 0, row < lax.axis_size("row") - 1
    has_left, has_right = col > 0, col < lax.axis_size("col") - 1
    up, down, left, right = {"row": row - 1}, {"row": row + 1}, {"col": col - 1}, {"col": col + 1}
    other = {"die": 1 - die}
    near = ((has_up, up), (has_down, down), (has_left, left), (has_right, right))

    pad[...] = jnp.zeros_like(pad)
    own = x_ref[...]
    pad[:, h : h + a, h : h + b] = jax.nn.sigmoid(own) if is_seed else own

    barrier = pltpu.get_barrier_semaphore()
    for there, device in near:
        @pl.when(there)
        def _(device=device):
            pl.semaphore_signal(barrier, inc=1, device_id=device, device_id_type=pl.DeviceIdType.MESH)
    pl.semaphore_signal(barrier, inc=1, device_id=other, device_id_type=pl.DeviceIdType.MESH)
    count = jnp.int32(1)
    for there, _ in near:
        count = count + there.astype(jnp.int32)
    pl.semaphore_wait(barrier, count)

    def copy(number, src, dst, device):
        return pltpu.make_async_remote_copy(
            src_ref=src, dst_ref=dst, send_sem=send.at[number], recv_sem=recv.at[number],
            device_id=device, device_id_type=pl.DeviceIdType.MESH,
        )

    tops = (0, h, h + a)
    sizes = (h, a, h)

    def block(band, start, width):
        return pad.at[:, pl.ds(tops[band], sizes[band]), pl.ds(start, width)]

    to_up = copy(0, pad.at[:, pl.ds(h, h), pl.ds(h, b)], block(2, h, b), up)
    to_down = copy(1, pad.at[:, pl.ds(a, h), pl.ds(h, b)], block(0, h, b), down)
    to_left = [copy(2 + k, block(k, h, h), block(k, h + b, h), left) for k in range(3)]
    to_right = [copy(5 + k, block(k, b, h), block(k, 0, h), right) for k in range(3)]

    def start(there, c):
        @pl.when(there)
        def _():
            c.start()

    def ended(there, c):
        @pl.when(there)
        def _():
            c.wait_send()

    def arrived(there, c):
        @pl.when(there)
        def _():
            c.wait_recv()

    start(has_up, to_up)
    start(has_down, to_down)
    start(has_left, to_left[1])
    start(has_right, to_right[1])

    def across_bands(t):
        span = jnp.broadcast_to(across_ref[pl.ds(t, 1), :], (a, a + 2 * h))
        head, rest = two_halves(pltpu.roll(span, 0, 1, stride=1, stride_axis=0))
        lines = pl.ds(t * a, a)
        w = a + 2 * h
        a_cat[lines, 0:w] = head
        a_cat[lines, w : 2 * w] = head
        a_cat[lines, 2 * w : 3 * w] = rest

    def down_bands(t):
        w = b + 2 * h
        span = jnp.broadcast_to(down_ref[pl.ds(t, 1), :], (h, 3 * h))
        head, rest = two_halves(pltpu.roll(span, 0, 1, stride=1, stride_axis=0))
        for part in range(3):
            piece = rest if part == 1 else head
            for k in range(b // h):
                lo, hi = k * h, k * h + 3 * h
                lines = pl.ds(k * h, h)
                d_cat[t, lines, part * w + lo : part * w + hi] = piece
                if lo:
                    d_cat[t, lines, part * w : part * w + lo] = jnp.zeros((h, lo), jnp.bfloat16)
                if hi < w:
                    d_cat[t, lines, part * w + hi : part * w + w] = jnp.zeros((h, w - hi), jnp.bfloat16)

    for t in range(terms):
        across_bands(t)
    arrived(has_down, to_up)
    for c, there in ((to_left[2], has_left), (to_right[2], has_right)):
        start(jnp.logical_and(has_down, there), c)
    arrived(has_up, to_down)
    for c, there in ((to_left[0], has_left), (to_right[0], has_right)):
        start(jnp.logical_and(has_up, there), c)
    for t in range(terms):
        down_bands(t)
    rows_of = (has_up, None, has_down)
    for k in range(3):
        for there, c in ((has_right, to_left[k]), (has_left, to_right[k])):
            arrived(there if k == 1 else jnp.logical_and(rows_of[k], there), c)

    w0, w1 = a + 2 * h, b + 2 * h
    for e in range(here):
        head, rest = two_halves(pad[e])
        cols = pl.ds(e * w1, w1)
        p_cat[0:w0, cols] = head
        p_cat[w0 : 2 * w0, cols] = rest
        p_cat[2 * w0 : 3 * w0, cols] = head

    def across(n, carry):
        cols = pl.ds(pl.multiple_of(n * 256, 256), 256)
        y_all[:, cols] = jnp.dot(a_cat[...], p_cat[:, cols], preferred_element_type=jnp.float32)
        return carry

    lax.fori_loop(0, here * w1 // 256, across, 0)
    acc[...] = jnp.zeros_like(acc)

    def along(t, carry):
        lines = pl.ds(pl.multiple_of(t * a, a), a)
        rows = jnp.concatenate([y_all[lines, e * w1 : (e + 1) * w1] for e in range(here)], axis=0)
        head, rest = two_halves(rows)
        z = lax.dot_general(
            jnp.concatenate([head, head, rest], axis=1), d_cat[t],
            (((1,), (1,)), ((), ())), preferred_element_type=jnp.float32,
        )
        for d in range(acc.shape[0]):
            total = acc[d]
            for e in range(here):
                total = total + mix_ref[t, d * here + e] * z[e * a : (e + 1) * a]
            acc[d] = total
        return carry

    lax.fori_loop(0, terms, along, 0)
    share = copy(8, acc.at[pl.ds((1 - die) * here, here)], got, other)
    share.start()
    for there, c in ((has_up, to_up), (has_down, to_down), (has_left, to_left[1]), (has_right, to_right[1])):
        ended(there, c)
    for k in (0, 2):
        for there, c in ((has_left, to_left[k]), (has_right, to_right[k])):
            ended(jnp.logical_and(rows_of[k], there), c)
    share.wait()
    out_ref[...] = acc[pl.ds(die * here, here)] + got[...]


def bases(taps):
    return jnp.pad(taps, ((0, 0), (1, 3 * HALO - 1 - taps.shape[1])))


def stage(fields, across_taps, down_taps, mix, is_seed):
    here, a, b = fields.shape
    terms, dies, _ = mix.shape
    w0, w1 = a + 2 * HALO, b + 2 * HALO
    vmem = pl.BlockSpec(memory_space=pltpu.VMEM)
    return pl.pallas_call(
        functools.partial(stage_kernel, is_seed),
        out_shape=jax.ShapeDtypeStruct(fields.shape, jnp.float32),
        in_specs=[vmem, vmem, vmem, pl.BlockSpec(memory_space=pltpu.SMEM)],
        out_specs=vmem,
        scratch_shapes=[
            pltpu.VMEM((here, w0, w1), jnp.float32),
            pltpu.VMEM((terms * a, 3 * w0), jnp.bfloat16),
            pltpu.VMEM((terms, b, 3 * w1), jnp.bfloat16),
            pltpu.VMEM((3 * w0, here * w1), jnp.bfloat16),
            pltpu.VMEM((terms * a, here * w1), jnp.float32),
            pltpu.VMEM((dies, a, b), jnp.float32),
            pltpu.VMEM((here, a, b), jnp.float32),
            pltpu.SemaphoreType.DMA((9,)),
            pltpu.SemaphoreType.DMA((9,)),
        ],
        compiler_params=pltpu.CompilerParams(
            collective_id=1 if is_seed else 0, has_side_effects=True, vmem_limit_bytes=48 * 2**20
        ),
    )(fields, bases(across_taps), bases(down_taps), mix.reshape(terms, dies * here))


def tiles_to_map(patch_totals_acc, tiles_down):
    dies_here, tile_total, cell_count = patch_totals_acc.shape
    mesh_layout = patch_totals_acc.reshape(
        dies_here, tile_total // tiles_down, tiles_down, PATCH_SIDE, PATCH_SIDE
    )
    return mesh_layout.transpose(0, 1, 3, 2, 4).reshape(
        dies_here, tile_total // tiles_down * PATCH_SIDE, tiles_down * PATCH_SIDE
    )


def map_to_tiles(source, tiles_down):
    dies_here, rows_all, cols_all = source.shape
    mesh_layout = source.reshape(
        dies_here, rows_all // PATCH_SIDE, PATCH_SIDE, tiles_down, PATCH_SIDE
    )
    return mesh_layout.transpose(0, 1, 3, 2, 4).reshape(dies_here, -1, PATCH_SIDE * PATCH_SIDE)


def local(parcel_patch, target_unit, target_patch, across_taps, down_taps, source_heated_mixing):
    dies_here, blocks_here, cells_tile = parcel_patch.shape
    devices_grid = lax.axis_size(("row", "col"))
    capacity = max(2, 2 * blocks_here // devices_grid)
    tiles_down = UNIT_MESH_Y // PATCH_SIDE
    destination = target_unit[:, :, 0]
    columns = jnp.arange(devices_grid, dtype=jnp.int32)
    same = destination[:, :, None] == destination[:, None, :]
    lines = jnp.arange(blocks_here, dtype=jnp.int32)
    earlier = lines[None, :] < lines[:, None]
    position = jnp.sum((same & earlier[None]).astype(jnp.int32), axis=2)
    slot_index = destination * capacity + position
    slots = jnp.arange(devices_grid * capacity, dtype=jnp.int32)
    place = (slot_index[:, :, None] == slots).astype(jnp.float32)
    outgoing = jnp.einsum("kbs,kbc->ksc", place, parcel_patch, precision=high)
    labels = jnp.sum(place * (target_patch.astype(jnp.float32) + 1.0)[:, :, None], axis=1) - 1.0
    arrived, arrived_tile = (
        lax.all_to_all(
            outgoing.reshape(dies_here, devices_grid, capacity, cells_tile),
            ("row", "col"),
            split_axis=1,
            concat_axis=1,
            tiled=True,
        ),
        lax.all_to_all(
            labels.reshape(dies_here, devices_grid, capacity),
            ("row", "col"),
            split_axis=1,
            concat_axis=1,
            tiled=True,
        ),
    )
    incoming = arrived.reshape(dies_here, -1, cells_tile)
    target = arrived_tile.reshape(dies_here, -1).astype(jnp.int32)
    chosen = (target[:, :, None] == lines).astype(jnp.float32)
    patch_totals_acc = jnp.einsum("kst,ksc->ktc", chosen, incoming, precision=high)
    wattage_field = tiles_to_map(patch_totals_acc, tiles_down)
    first_die = lax.axis_index("die") * dies_here
    own_columns = lax.dynamic_slice_in_dim(source_heated_mixing, first_die, dies_here, 2)
    own_rows = lax.dynamic_slice_in_dim(source_heated_mixing, first_die, dies_here, 1)
    chip_heat_increase = stage(wattage_field, across_taps, down_taps, own_columns, False)
    adjoint_field_map = stage(
        chip_heat_increase, across_taps[:, ::-1], down_taps[:, ::-1], own_rows.transpose(0, 2, 1), True
    )
    adjoint_patches = map_to_tiles(adjoint_field_map, tiles_down)
    answers = jnp.einsum("kst,ktc->ksc", chosen, adjoint_patches, precision=high)
    returned = lax.all_to_all(
        answers.reshape(dies_here, devices_grid, capacity, cells_tile),
        ("row", "col"),
        split_axis=1,
        concat_axis=1,
        tiled=True,
    )
    block_power_slopes = jnp.einsum(
        "kbs,ksc->kbc", place, returned.reshape(dies_here, -1, cells_tile), precision=high
    )
    return (chip_heat_increase, block_power_slopes)


def solution(mesh):
    placed = (
        P("die", ("row", "col"), None),
        P("die", ("row", "col"), None),
        P("die", ("row", "col")),
        P(),
        P(),
        P(),
    )
    return jax.shard_map(
        local,
        mesh=mesh,
        in_specs=placed,
        out_specs=(P("die", "row", "col"), P("die", ("row", "col"), None)),
        check_vma=False,
    )
```

```python
import functools

import jax
import jax.numpy as jnp
from jax import lax
from jax.experimental import pallas as pl
from jax.experimental.pallas import tpu as pltpu
from jax.sharding import PartitionSpec as P

PATCH_SIDE = 16
UNIT_MESH_X = 128
UNIT_MESH_Y = 256
HALO = 128


high = lax.Precision.HIGH


def two_halves(values):
    head = values.astype(jnp.bfloat16)
    return head, (values - head.astype(jnp.float32)).astype(jnp.bfloat16)


def stage_kernel(
    is_seed, x_ref, across_ref, down_ref, mix_ref, out_ref,
    pad, a_cat, d_cat, p_cat, y_all, acc, got, send, recv,
):
    here, a, b = x_ref.shape
    terms = across_ref.shape[0]
    h = HALO
    row, col, die = lax.axis_index("row"), lax.axis_index("col"), lax.axis_index("die")
    has_up, has_down = row > 0, row < lax.axis_size("row") - 1
    has_left, has_right = col > 0, col < lax.axis_size("col") - 1
    up, down, left, right = {"row": row - 1}, {"row": row + 1}, {"col": col - 1}, {"col": col + 1}
    other = {"die": 1 - die}
    near = ((has_up, up), (has_down, down), (has_left, left), (has_right, right))

    pad[...] = jnp.zeros_like(pad)
    own = x_ref[...]
    pad[:, h : h + a, h : h + b] = jax.nn.sigmoid(own) if is_seed else own

    barrier = pltpu.get_barrier_semaphore()
    for there, device in near:
        @pl.when(there)
        def _(device=device):
            pl.semaphore_signal(barrier, inc=1, device_id=device, device_id_type=pl.DeviceIdType.MESH)
    pl.semaphore_signal(barrier, inc=1, device_id=other, device_id_type=pl.DeviceIdType.MESH)
    count = jnp.int32(1)
    for there, _ in near:
        count = count + there.astype(jnp.int32)
    pl.semaphore_wait(barrier, count)

    def copy(number, src, dst, device):
        return pltpu.make_async_remote_copy(
            src_ref=src, dst_ref=dst, send_sem=send.at[number], recv_sem=recv.at[number],
            device_id=device, device_id_type=pl.DeviceIdType.MESH,
        )

    tops = (0, h, h + a)
    sizes = (h, a, h)

    def block(band, start, width):
        return pad.at[:, pl.ds(tops[band], sizes[band]), pl.ds(start, width)]

    to_up = copy(0, pad.at[:, pl.ds(h, h), pl.ds(h, b)], block(2, h, b), up)
    to_down = copy(1, pad.at[:, pl.ds(a, h), pl.ds(h, b)], block(0, h, b), down)
    to_left = [copy(2 + k, block(k, h, h), block(k, h + b, h), left) for k in range(3)]
    to_right = [copy(5 + k, block(k, b, h), block(k, 0, h), right) for k in range(3)]

    def start(there, c):
        @pl.when(there)
        def _():
            c.start()

    def ended(there, c):
        @pl.when(there)
        def _():
            c.wait_send()

    def arrived(there, c):
        @pl.when(there)
        def _():
            c.wait_recv()

    start(has_up, to_up)
    start(has_down, to_down)
    start(has_left, to_left[1])
    start(has_right, to_right[1])

    def across_bands(t):
        span = jnp.broadcast_to(across_ref[pl.ds(t, 1), :], (a, a + 2 * h))
        head, rest = two_halves(pltpu.roll(span, 0, 1, stride=1, stride_axis=0))
        lines = pl.ds(t * a, a)
        w = a + 2 * h
        a_cat[lines, 0:w] = head
        a_cat[lines, w : 2 * w] = head
        a_cat[lines, 2 * w : 3 * w] = rest

    def down_bands(t):
        w = b + 2 * h
        span = jnp.broadcast_to(down_ref[pl.ds(t, 1), :], (h, 3 * h))
        head, rest = two_halves(pltpu.roll(span, 0, 1, stride=1, stride_axis=0))
        for part in range(3):
            piece = rest if part == 1 else head
            for k in range(b // h):
                lo, hi = k * h, k * h + 3 * h
                lines = pl.ds(k * h, h)
                d_cat[t, lines, part * w + lo : part * w + hi] = piece
                if lo:
                    d_cat[t, lines, part * w : part * w + lo] = jnp.zeros((h, lo), jnp.bfloat16)
                if hi < w:
                    d_cat[t, lines, part * w + hi : part * w + w] = jnp.zeros((h, w - hi), jnp.bfloat16)

    for t in range(terms):
        across_bands(t)
    arrived(has_down, to_up)
    for c, there in ((to_left[2], has_left), (to_right[2], has_right)):
        start(jnp.logical_and(has_down, there), c)
    arrived(has_up, to_down)
    for c, there in ((to_left[0], has_left), (to_right[0], has_right)):
        start(jnp.logical_and(has_up, there), c)
    for t in range(terms):
        down_bands(t)
    rows_of = (has_up, None, has_down)
    for k in range(3):
        for there, c in ((has_right, to_left[k]), (has_left, to_right[k])):
            arrived(there if k == 1 else jnp.logical_and(rows_of[k], there), c)

    w0, w1 = a + 2 * h, b + 2 * h
    for e in range(here):
        head, rest = two_halves(pad[e])
        cols = pl.ds(e * w1, w1)
        p_cat[0:w0, cols] = head
        p_cat[w0 : 2 * w0, cols] = rest
        p_cat[2 * w0 : 3 * w0, cols] = head

    def across(n, carry):
        cols = pl.ds(pl.multiple_of(n * 256, 256), 256)
        y_all[:, cols] = jnp.dot(a_cat[...], p_cat[:, cols], preferred_element_type=jnp.float32)
        return carry

    lax.fori_loop(0, here * w1 // 256, across, 0)
    acc[...] = jnp.zeros_like(acc)

    def along(t, carry):
        lines = pl.ds(pl.multiple_of(t * a, a), a)
        rows = jnp.concatenate([y_all[lines, e * w1 : (e + 1) * w1] for e in range(here)], axis=0)
        head, rest = two_halves(rows)
        z = lax.dot_general(
            jnp.concatenate([head, head, rest], axis=1), d_cat[t],
            (((1,), (1,)), ((), ())), preferred_element_type=jnp.float32,
        )
        for d in range(acc.shape[0]):
            total = acc[d]
            for e in range(here):
                total = total + mix_ref[t, d * here + e] * z[e * a : (e + 1) * a]
            acc[d] = total
        return carry

    lax.fori_loop(0, terms, along, 0)
    share = copy(8, acc.at[pl.ds((1 - die) * here, here)], got, other)
    share.start()
    for there, c in ((has_up, to_up), (has_down, to_down), (has_left, to_left[1]), (has_right, to_right[1])):
        ended(there, c)
    for k in (0, 2):
        for there, c in ((has_left, to_left[k]), (has_right, to_right[k])):
            ended(jnp.logical_and(rows_of[k], there), c)
    share.wait()
    out_ref[...] = acc[pl.ds(die * here, here)] + got[...]


def bases(taps):
    return jnp.pad(taps, ((0, 0), (1, 3 * HALO - 1 - taps.shape[1])))


def stage(fields, across_taps, down_taps, mix, is_seed):
    here, a, b = fields.shape
    terms, dies, _ = mix.shape
    w0, w1 = a + 2 * HALO, b + 2 * HALO
    vmem = pl.BlockSpec(memory_space=pltpu.VMEM)
    return pl.pallas_call(
        functools.partial(stage_kernel, is_seed),
        out_shape=jax.ShapeDtypeStruct(fields.shape, jnp.float32),
        in_specs=[vmem, vmem, vmem, pl.BlockSpec(memory_space=pltpu.SMEM)],
        out_specs=vmem,
        scratch_shapes=[
            pltpu.VMEM((here, w0, w1), jnp.float32),
            pltpu.VMEM((terms * a, 3 * w0), jnp.bfloat16),
            pltpu.VMEM((terms, b, 3 * w1), jnp.bfloat16),
            pltpu.VMEM((3 * w0, here * w1), jnp.bfloat16),
            pltpu.VMEM((terms * a, here * w1), jnp.float32),
            pltpu.VMEM((dies, a, b), jnp.float32),
            pltpu.VMEM((here, a, b), jnp.float32),
            pltpu.SemaphoreType.DMA((9,)),
            pltpu.SemaphoreType.DMA((9,)),
        ],
        compiler_params=pltpu.CompilerParams(
            collective_id=1 if is_seed else 0, has_side_effects=True, vmem_limit_bytes=48 * 2**20
        ),
    )(fields, bases(across_taps), bases(down_taps), mix.reshape(terms, dies * here))


def swap_kernel(*refs):
    count = (len(refs) - 3) // 2
    sources, landed = refs[:count], refs[count : 2 * count]
    send, recv, keep = refs[2 * count :]
    across = lax.axis_size("col")
    peers = across * lax.axis_size("row")
    me = lax.axis_index("row") * across + lax.axis_index("col")
    barrier = pltpu.get_barrier_semaphore()

    def place(number):
        return {"row": number // across, "col": number % across}

    def greet(i, carry):
        pl.semaphore_signal(
            barrier, inc=1, device_id=place((me + i) % peers), device_id_type=pl.DeviceIdType.MESH
        )
        return carry

    def copies(i):
        to = (me + i) % peers
        return [
            pltpu.make_async_remote_copy(
                src_ref=src.at[:, to], dst_ref=dst.at[:, me],
                send_sem=send.at[k, i], recv_sem=recv.at[k, i],
                device_id=place(to), device_id_type=pl.DeviceIdType.MESH,
            )
            for k, (src, dst) in enumerate(zip(sources, landed))
        ]

    def begin(i, carry):
        for c in copies(i):
            c.start()
        return carry

    def finish(i, carry):
        for c in copies(i):
            c.wait()
        return carry

    lax.fori_loop(1, peers, greet, 0)
    pl.semaphore_wait(barrier, peers - 1)
    lax.fori_loop(1, peers, begin, 0)
    stay = [
        pltpu.make_async_copy(src.at[:, me], dst.at[:, me], keep.at[k])
        for k, (src, dst) in enumerate(zip(sources, landed))
    ]
    for c in stay:
        c.start()
    for c in stay:
        c.wait()
    lax.fori_loop(1, peers, finish, 0)


def swap(arrays, number):
    count, peers = len(arrays), arrays[0].shape[1]
    vmem = pl.BlockSpec(memory_space=pltpu.VMEM)
    return pl.pallas_call(
        swap_kernel,
        out_shape=[jax.ShapeDtypeStruct(x.shape, x.dtype) for x in arrays],
        in_specs=[vmem] * count,
        out_specs=[vmem] * count,
        scratch_shapes=[
            pltpu.SemaphoreType.DMA((count, peers)),
            pltpu.SemaphoreType.DMA((count, peers)),
            pltpu.SemaphoreType.DMA((count,)),
        ],
        compiler_params=pltpu.CompilerParams(
            collective_id=number, has_side_effects=True, vmem_limit_bytes=24 * 2**20
        ),
    )(*arrays)


def tiles_to_map(patch_totals_acc, tiles_down):
    dies_here, tile_total, cell_count = patch_totals_acc.shape
    mesh_layout = patch_totals_acc.reshape(
        dies_here, tile_total // tiles_down, tiles_down, PATCH_SIDE, PATCH_SIDE
    )
    return mesh_layout.transpose(0, 1, 3, 2, 4).reshape(
        dies_here, tile_total // tiles_down * PATCH_SIDE, tiles_down * PATCH_SIDE
    )


def map_to_tiles(source, tiles_down):
    dies_here, rows_all, cols_all = source.shape
    mesh_layout = source.reshape(
        dies_here, rows_all // PATCH_SIDE, PATCH_SIDE, tiles_down, PATCH_SIDE
    )
    return mesh_layout.transpose(0, 1, 3, 2, 4).reshape(dies_here, -1, PATCH_SIDE * PATCH_SIDE)


def local(parcel_patch, target_unit, target_patch, across_taps, down_taps, source_heated_mixing):
    dies_here, blocks_here, cells_tile = parcel_patch.shape
    devices_grid = lax.axis_size(("row", "col"))
    capacity = max(2, 2 * blocks_here // devices_grid)
    tiles_down = UNIT_MESH_Y // PATCH_SIDE
    destination = target_unit[:, :, 0]
    columns = jnp.arange(devices_grid, dtype=jnp.int32)
    same = destination[:, :, None] == destination[:, None, :]
    lines = jnp.arange(blocks_here, dtype=jnp.int32)
    earlier = lines[None, :] < lines[:, None]
    position = jnp.sum((same & earlier[None]).astype(jnp.int32), axis=2)
    slot_index = destination * capacity + position
    slots = jnp.arange(devices_grid * capacity, dtype=jnp.int32)
    place = (slot_index[:, :, None] == slots).astype(jnp.float32)
    outgoing = jnp.einsum("kbs,kbc->ksc", place, parcel_patch, precision=high)
    labels = jnp.sum(place * (target_patch.astype(jnp.float32) + 1.0)[:, :, None], axis=1) - 1.0
    span = dies_here * capacity
    rows = labels.reshape(dies_here, devices_grid, capacity).transpose(1, 0, 2).reshape(1, devices_grid, 1, span)
    rows = jnp.pad(rows, ((0, 0), (0, 0), (0, 0), (0, 128 - span)))
    arrived, arrived_rows = swap(
        (outgoing.reshape(dies_here, devices_grid, capacity, cells_tile), rows), 2
    )
    incoming = arrived.reshape(dies_here, -1, cells_tile)
    arrived_tile = arrived_rows[0, :, 0, :span].reshape(devices_grid, dies_here, capacity).transpose(1, 0, 2)
    target = arrived_tile.reshape(dies_here, -1).astype(jnp.int32)
    chosen = (target[:, :, None] == lines).astype(jnp.float32)
    patch_totals_acc = jnp.einsum("kst,ksc->ktc", chosen, incoming, precision=high)
    wattage_field = tiles_to_map(patch_totals_acc, tiles_down)
    first_die = lax.axis_index("die") * dies_here
    own_columns = lax.dynamic_slice_in_dim(source_heated_mixing, first_die, dies_here, 2)
    own_rows = lax.dynamic_slice_in_dim(source_heated_mixing, first_die, dies_here, 1)
    chip_heat_increase = stage(wattage_field, across_taps, down_taps, own_columns, False)
    adjoint_field_map = stage(
        chip_heat_increase, across_taps[:, ::-1], down_taps[:, ::-1], own_rows.transpose(0, 2, 1), True
    )
    adjoint_patches = map_to_tiles(adjoint_field_map, tiles_down)
    answers = jnp.einsum("kst,ktc->ksc", chosen, adjoint_patches, precision=high)
    (returned,) = swap((answers.reshape(dies_here, devices_grid, capacity, cells_tile),), 3)
    block_power_slopes = jnp.einsum(
        "kbs,ksc->kbc", place, returned.reshape(dies_here, -1, cells_tile), precision=high
    )
    return (chip_heat_increase, block_power_slopes)


def solution(mesh):
    placed = (
        P("die", ("row", "col"), None),
        P("die", ("row", "col"), None),
        P("die", ("row", "col")),
        P(),
        P(),
        P(),
    )
    return jax.shard_map(
        local,
        mesh=mesh,
        in_specs=placed,
        out_specs=(P("die", "row", "col"), P("die", ("row", "col"), None)),
        check_vma=False,
    )
```

```python
import functools

import jax
import jax.numpy as jnp
from jax import lax
from jax.experimental import pallas as pl
from jax.experimental.pallas import tpu as pltpu
from jax.sharding import PartitionSpec as P

PATCH_SIDE = 16
UNIT_MESH_X = 128
UNIT_MESH_Y = 256
HALO = 128


high = lax.Precision.HIGH


def two_halves(values):
    head = values.astype(jnp.bfloat16)
    return head, (values - head.astype(jnp.float32)).astype(jnp.bfloat16)


def stage_kernel(
    is_seed, x_ref, across_ref, down_ref, mix_ref, out_ref,
    pad, a_cat, d_cat, p_cat, y_all, acc, got, send, recv,
):
    here, a, b = x_ref.shape
    terms = across_ref.shape[0]
    h = HALO
    row, col, die = lax.axis_index("row"), lax.axis_index("col"), lax.axis_index("die")
    has_up, has_down = row > 0, row < lax.axis_size("row") - 1
    has_left, has_right = col > 0, col < lax.axis_size("col") - 1
    up, down, left, right = {"row": row - 1}, {"row": row + 1}, {"col": col - 1}, {"col": col + 1}
    other = {"die": 1 - die}
    near = ((has_up, up), (has_down, down), (has_left, left), (has_right, right))

    pad[...] = jnp.zeros_like(pad)
    own = x_ref[...]
    pad[:, h : h + a, h : h + b] = jax.nn.sigmoid(own) if is_seed else own

    barrier = pltpu.get_barrier_semaphore()
    for there, device in near:
        @pl.when(there)
        def _(device=device):
            pl.semaphore_signal(barrier, inc=1, device_id=device, device_id_type=pl.DeviceIdType.MESH)
    pl.semaphore_signal(barrier, inc=1, device_id=other, device_id_type=pl.DeviceIdType.MESH)
    count = jnp.int32(1)
    for there, _ in near:
        count = count + there.astype(jnp.int32)
    pl.semaphore_wait(barrier, count)

    def copy(number, src, dst, device):
        return pltpu.make_async_remote_copy(
            src_ref=src, dst_ref=dst, send_sem=send.at[number], recv_sem=recv.at[number],
            device_id=device, device_id_type=pl.DeviceIdType.MESH,
        )

    tops = (0, h, h + a)
    sizes = (h, a, h)

    def block(band, start, width):
        return pad.at[:, pl.ds(tops[band], sizes[band]), pl.ds(start, width)]

    to_up = copy(0, pad.at[:, pl.ds(h, h), pl.ds(h, b)], block(2, h, b), up)
    to_down = copy(1, pad.at[:, pl.ds(a, h), pl.ds(h, b)], block(0, h, b), down)
    to_left = [copy(2 + k, block(k, h, h), block(k, h + b, h), left) for k in range(3)]
    to_right = [copy(5 + k, block(k, b, h), block(k, 0, h), right) for k in range(3)]

    def start(there, c):
        @pl.when(there)
        def _():
            c.start()

    def ended(there, c):
        @pl.when(there)
        def _():
            c.wait_send()

    def arrived(there, c):
        @pl.when(there)
        def _():
            c.wait_recv()

    start(has_up, to_up)
    start(has_down, to_down)
    start(has_left, to_left[1])
    start(has_right, to_right[1])

    def across_bands(t):
        span = jnp.broadcast_to(across_base[t : t + 1, :], (a, a + 2 * h))
        head, rest = two_halves(pltpu.roll(span, 0, 1, stride=1, stride_axis=0))
        lines = pl.ds(t * a, a)
        w = a + 2 * h
        a_cat[lines, 0:w] = head
        a_cat[lines, w : 2 * w] = head
        a_cat[lines, 2 * w : 3 * w] = rest

    def down_bands(t):
        w = b + 2 * h
        span = jnp.broadcast_to(down_base[t : t + 1, :], (h, 3 * h))
        head, rest = two_halves(pltpu.roll(span, 0, 1, stride=1, stride_axis=0))
        for part in range(3):
            piece = rest if part == 1 else head
            for k in range(b // h):
                lo, hi = k * h, k * h + 3 * h
                lines = pl.ds(k * h, h)
                d_cat[t, lines, part * w + lo : part * w + hi] = piece
                if lo:
                    d_cat[t, lines, part * w : part * w + lo] = jnp.zeros((h, lo), jnp.bfloat16)
                if hi < w:
                    d_cat[t, lines, part * w + hi : part * w + w] = jnp.zeros((h, w - hi), jnp.bfloat16)

    def base(taps_ref):
        taps = taps_ref.shape[1]
        k = lax.broadcasted_iota(jnp.int32, (taps, 3 * h), 0)
        u = lax.broadcasted_iota(jnp.int32, (taps, 3 * h), 1)
        pick = (u == (taps - k if is_seed else k + 1)).astype(jnp.float32)
        return jnp.dot(
            taps_ref[...], pick, precision=lax.Precision.HIGHEST, preferred_element_type=jnp.float32
        )

    across_base, down_base = base(across_ref), base(down_ref)
    for t in range(terms):
        across_bands(t)
    arrived(has_down, to_up)
    for c, there in ((to_left[2], has_left), (to_right[2], has_right)):
        start(jnp.logical_and(has_down, there), c)
    arrived(has_up, to_down)
    for c, there in ((to_left[0], has_left), (to_right[0], has_right)):
        start(jnp.logical_and(has_up, there), c)
    w0, w1 = a + 2 * h, b + 2 * h

    def fill(e, source, at, width):
        head, rest = two_halves(pad[e, :, source : source + width])
        cols = slice(e * w1 + at, e * w1 + at + width)
        p_cat[0:w0, cols] = head
        p_cat[w0 : 2 * w0, cols] = rest
        p_cat[2 * w0 : 3 * w0, cols] = head

    def across(at, width):
        cols = slice(at, at + width)
        y_all[:, cols] = jnp.dot(a_cat[...], p_cat[:, cols], preferred_element_type=jnp.float32)

    for e in range(here):
        fill(e, h, 0, b)
        across(e * w1, b)
    for t in range(terms):
        down_bands(t)
    rows_of = (has_up, None, has_down)
    for k in range(3):
        for there, c in ((has_right, to_left[k]), (has_left, to_right[k])):
            arrived(there if k == 1 else jnp.logical_and(rows_of[k], there), c)
    for e in range(here):
        fill(e, 0, b, h)
        fill(e, h + b, b + h, h)
        across(e * w1 + b, 2 * h)
    acc[...] = jnp.zeros_like(acc)

    def weight(t, d, e):
        mine = die * here + e
        return mix_ref[t, mine * acc.shape[0] + d if is_seed else d * acc.shape[0] + mine]

    def along(t, carry):
        lines = pl.ds(pl.multiple_of(t * a, a), a)
        rows = jnp.concatenate(
            [
                jnp.concatenate(
                    [
                        y_all[lines, e * w1 + b : e * w1 + b + h],
                        y_all[lines, e * w1 : e * w1 + b],
                        y_all[lines, e * w1 + b + h : (e + 1) * w1],
                    ],
                    axis=1,
                )
                for e in range(here)
            ],
            axis=0,
        )
        head, rest = two_halves(rows)
        z = lax.dot_general(
            jnp.concatenate([head, head, rest], axis=1), d_cat[t],
            (((1,), (1,)), ((), ())), preferred_element_type=jnp.float32,
        )
        for d in range(acc.shape[0]):
            total = acc[d]
            for e in range(here):
                total = total + weight(t, d, e) * z[e * a : (e + 1) * a]
            acc[d] = total
        return carry

    lax.fori_loop(0, terms, along, 0)
    share = copy(8, acc.at[pl.ds((1 - die) * here, here)], got, other)
    share.start()
    for there, c in ((has_up, to_up), (has_down, to_down), (has_left, to_left[1]), (has_right, to_right[1])):
        ended(there, c)
    for k in (0, 2):
        for there, c in ((has_left, to_left[k]), (has_right, to_right[k])):
            ended(jnp.logical_and(rows_of[k], there), c)
    share.wait()
    out_ref[...] = acc[pl.ds(die * here, here)] + got[...]


def stage(fields, across_taps, down_taps, mix, is_seed):
    here, a, b = fields.shape
    terms, dies, _ = mix.shape
    w0, w1 = a + 2 * HALO, b + 2 * HALO
    vmem = pl.BlockSpec(memory_space=pltpu.VMEM)
    return pl.pallas_call(
        functools.partial(stage_kernel, is_seed),
        out_shape=jax.ShapeDtypeStruct(fields.shape, jnp.float32),
        in_specs=[vmem, vmem, vmem, pl.BlockSpec(memory_space=pltpu.SMEM)],
        out_specs=vmem,
        scratch_shapes=[
            pltpu.VMEM((here, w0, w1), jnp.float32),
            pltpu.VMEM((terms * a, 3 * w0), jnp.bfloat16),
            pltpu.VMEM((terms, b, 3 * w1), jnp.bfloat16),
            pltpu.VMEM((3 * w0, here * w1), jnp.bfloat16),
            pltpu.VMEM((terms * a, here * w1), jnp.float32),
            pltpu.VMEM((dies, a, b), jnp.float32),
            pltpu.VMEM((here, a, b), jnp.float32),
            pltpu.SemaphoreType.DMA((9,)),
            pltpu.SemaphoreType.DMA((9,)),
        ],
        compiler_params=pltpu.CompilerParams(
            collective_id=1 if is_seed else 0, has_side_effects=True, vmem_limit_bytes=48 * 2**20
        ),
    )(fields, across_taps, down_taps, mix.reshape(terms, dies * dies))


def swap_kernel(*refs):
    count = (len(refs) - 3) // 2
    sources, landed = refs[:count], refs[count : 2 * count]
    send, recv, keep = refs[2 * count :]
    across = lax.axis_size("col")
    peers = across * lax.axis_size("row")
    me = lax.axis_index("row") * across + lax.axis_index("col")
    barrier = pltpu.get_barrier_semaphore()

    def place(number):
        return {"row": number // across, "col": number % across}

    def greet(i, carry):
        pl.semaphore_signal(
            barrier, inc=1, device_id=place((me + i) % peers), device_id_type=pl.DeviceIdType.MESH
        )
        return carry

    def copies(i):
        to = (me + i) % peers
        return [
            pltpu.make_async_remote_copy(
                src_ref=src.at[:, to], dst_ref=dst.at[:, me],
                send_sem=send.at[k, i], recv_sem=recv.at[k, i],
                device_id=place(to), device_id_type=pl.DeviceIdType.MESH,
            )
            for k, (src, dst) in enumerate(zip(sources, landed))
        ]

    def begin(i, carry):
        for c in copies((i + peers // 2 - 2) % (peers - 1) + 1):
            c.start()
        return carry

    def finish(i, carry):
        for c in copies(i):
            c.wait()
        return carry

    lax.fori_loop(1, peers, greet, 0)
    pl.semaphore_wait(barrier, peers - 1)
    lax.fori_loop(1, peers, begin, 0)
    stay = [
        pltpu.make_async_copy(src.at[:, me], dst.at[:, me], keep.at[k])
        for k, (src, dst) in enumerate(zip(sources, landed))
    ]
    for c in stay:
        c.start()
    for c in stay:
        c.wait()
    lax.fori_loop(1, peers, finish, 0)


def swap(arrays, number):
    count, peers = len(arrays), arrays[0].shape[1]
    vmem = pl.BlockSpec(memory_space=pltpu.VMEM)
    return pl.pallas_call(
        swap_kernel,
        out_shape=[jax.ShapeDtypeStruct(x.shape, x.dtype) for x in arrays],
        in_specs=[vmem] * count,
        out_specs=[vmem] * count,
        scratch_shapes=[
            pltpu.SemaphoreType.DMA((count, peers)),
            pltpu.SemaphoreType.DMA((count, peers)),
            pltpu.SemaphoreType.DMA((count,)),
        ],
        compiler_params=pltpu.CompilerParams(
            collective_id=number, has_side_effects=True, vmem_limit_bytes=24 * 2**20
        ),
    )(*arrays)


def tiles_to_map(patch_totals_acc, tiles_down):
    dies_here, tile_total, cell_count = patch_totals_acc.shape
    mesh_layout = patch_totals_acc.reshape(
        dies_here, tile_total // tiles_down, tiles_down, PATCH_SIDE, PATCH_SIDE
    )
    return mesh_layout.transpose(0, 1, 3, 2, 4).reshape(
        dies_here, tile_total // tiles_down * PATCH_SIDE, tiles_down * PATCH_SIDE
    )


def map_to_tiles(source, tiles_down):
    dies_here, rows_all, cols_all = source.shape
    mesh_layout = source.reshape(
        dies_here, rows_all // PATCH_SIDE, PATCH_SIDE, tiles_down, PATCH_SIDE
    )
    return mesh_layout.transpose(0, 1, 3, 2, 4).reshape(dies_here, -1, PATCH_SIDE * PATCH_SIDE)


def local(parcel_patch, target_unit, target_patch, across_taps, down_taps, source_heated_mixing):
    dies_here, blocks_here, cells_tile = parcel_patch.shape
    devices_grid = lax.axis_size(("row", "col"))
    capacity = max(2, 2 * blocks_here // devices_grid)
    tiles_down = UNIT_MESH_Y // PATCH_SIDE
    destination = target_unit[:, :, 0]
    columns = jnp.arange(devices_grid, dtype=jnp.int32)
    same = destination[:, :, None] == destination[:, None, :]
    lines = jnp.arange(blocks_here, dtype=jnp.int32)
    earlier = lines[None, :] < lines[:, None]
    position = jnp.sum((same & earlier[None]).astype(jnp.int32), axis=2)
    slot_index = destination * capacity + position
    slots = jnp.arange(devices_grid * capacity, dtype=jnp.int32)
    place = (slot_index[:, :, None] == slots).astype(jnp.float32)
    outgoing = jnp.einsum("kbs,kbc->ksc", place, parcel_patch, precision=high)
    labels = jnp.sum(place * (target_patch.astype(jnp.float32) + 1.0)[:, :, None], axis=1) - 1.0
    span = dies_here * capacity
    rows = labels.reshape(dies_here, devices_grid, capacity).transpose(1, 0, 2).reshape(1, devices_grid, 1, span)
    rows = jnp.pad(rows, ((0, 0), (0, 0), (0, 0), (0, 128 - span)))
    arrived, arrived_rows = swap(
        (outgoing.reshape(dies_here, devices_grid, capacity, cells_tile), rows), 2
    )
    incoming = arrived.reshape(dies_here, -1, cells_tile)
    arrived_tile = arrived_rows[0, :, 0, :span].reshape(devices_grid, dies_here, capacity).transpose(1, 0, 2)
    target = arrived_tile.reshape(dies_here, -1).astype(jnp.int32)
    chosen = (target[:, :, None] == lines).astype(jnp.float32)
    patch_totals_acc = jnp.einsum("kst,ksc->ktc", chosen, incoming, precision=high)
    wattage_field = tiles_to_map(patch_totals_acc, tiles_down)
    chip_heat_increase = stage(wattage_field, across_taps, down_taps, source_heated_mixing, False)
    adjoint_field_map = stage(chip_heat_increase, across_taps, down_taps, source_heated_mixing, True)
    adjoint_patches = map_to_tiles(adjoint_field_map, tiles_down)
    answers = jnp.einsum("kst,ktc->ksc", chosen, adjoint_patches, precision=high)
    (returned,) = swap((answers.reshape(dies_here, devices_grid, capacity, cells_tile),), 3)
    block_power_slopes = jnp.einsum(
        "kbs,ksc->kbc", place, returned.reshape(dies_here, -1, cells_tile), precision=high
    )
    return (chip_heat_increase, block_power_slopes)


def solution(mesh):
    placed = (
        P("die", ("row", "col"), None),
        P("die", ("row", "col"), None),
        P("die", ("row", "col")),
        P(),
        P(),
        P(),
    )
    return jax.shard_map(
        local,
        mesh=mesh,
        in_specs=placed,
        out_specs=(P("die", "row", "col"), P("die", ("row", "col"), None)),
        check_vma=False,
    )
```

```python
import functools

import jax
import jax.numpy as jnp
from jax import lax
from jax.experimental import pallas as pl
from jax.experimental.pallas import tpu as pltpu
from jax.sharding import PartitionSpec as P

PATCH_SIDE = 16
UNIT_MESH_X = 128
UNIT_MESH_Y = 256
HALO = 128


high = lax.Precision.HIGH


def two_halves(values):
    head = values.astype(jnp.bfloat16)
    return head, (values - head.astype(jnp.float32)).astype(jnp.bfloat16)


def stage_kernel(
    is_seed, x_ref, across_ref, down_ref, mix_ref, out_ref,
    pad, a_cat, d_cat, p_cat, y_all, acc, got, send, recv,
):
    here, a, b = x_ref.shape
    terms = across_ref.shape[0]
    h = HALO
    row, col, die = lax.axis_index("row"), lax.axis_index("col"), lax.axis_index("die")
    has_up, has_down = row > 0, row < lax.axis_size("row") - 1
    has_left, has_right = col > 0, col < lax.axis_size("col") - 1
    up, down, left, right = {"row": row - 1}, {"row": row + 1}, {"col": col - 1}, {"col": col + 1}
    other = {"die": 1 - die}
    near = ((has_up, up), (has_down, down), (has_left, left), (has_right, right))

    pad[...] = jnp.zeros_like(pad)
    own = x_ref[...]
    pad[:, h : h + a, h : h + b] = jax.nn.sigmoid(own) if is_seed else own

    barrier = pltpu.get_barrier_semaphore()
    for there, device in near:
        @pl.when(there)
        def _(device=device):
            pl.semaphore_signal(barrier, inc=1, device_id=device, device_id_type=pl.DeviceIdType.MESH)
    pl.semaphore_signal(barrier, inc=1, device_id=other, device_id_type=pl.DeviceIdType.MESH)
    count = jnp.int32(1)
    for there, _ in near:
        count = count + there.astype(jnp.int32)
    pl.semaphore_wait(barrier, count)

    def copy(number, src, dst, device):
        return pltpu.make_async_remote_copy(
            src_ref=src, dst_ref=dst, send_sem=send.at[number], recv_sem=recv.at[number],
            device_id=device, device_id_type=pl.DeviceIdType.MESH,
        )

    tops = (0, h, h + a)
    sizes = (h, a, h)

    def block(band, start, width):
        return pad.at[:, pl.ds(tops[band], sizes[band]), pl.ds(start, width)]

    to_up = copy(0, pad.at[:, pl.ds(h, h), pl.ds(h, b)], block(2, h, b), up)
    to_down = copy(1, pad.at[:, pl.ds(a, h), pl.ds(h, b)], block(0, h, b), down)
    to_left = [copy(2 + k, block(k, h, h), block(k, h + b, h), left) for k in range(3)]
    to_right = [copy(5 + k, block(k, b, h), block(k, 0, h), right) for k in range(3)]

    def start(there, c):
        @pl.when(there)
        def _():
            c.start()

    def ended(there, c):
        @pl.when(there)
        def _():
            c.wait_send()

    def arrived(there, c):
        @pl.when(there)
        def _():
            c.wait_recv()

    start(has_up, to_up)
    start(has_down, to_down)
    start(has_left, to_left[1])
    start(has_right, to_right[1])

    def across_bands(t):
        span = jnp.broadcast_to(across_base[t : t + 1, :], (a, a + 2 * h))
        head, rest = two_halves(pltpu.roll(span, 0, 1, stride=1, stride_axis=0))
        lines = pl.ds(t * a, a)
        w = a + 2 * h
        a_cat[lines, 0:w] = head
        a_cat[lines, w : 2 * w] = head
        a_cat[lines, 2 * w : 3 * w] = rest

    def down_bands(t):
        w = b + 2 * h
        span = jnp.broadcast_to(down_base[t : t + 1, :], (h, 3 * h))
        head, rest = two_halves(pltpu.roll(span, 0, 1, stride=1, stride_axis=0))
        for part in range(3):
            piece = rest if part == 1 else head
            for k in range(b // h):
                lo, hi = k * h, k * h + 3 * h
                lines = pl.ds(k * h, h)
                d_cat[t, lines, part * w + lo : part * w + hi] = piece
                if lo:
                    d_cat[t, lines, part * w : part * w + lo] = jnp.zeros((h, lo), jnp.bfloat16)
                if hi < w:
                    d_cat[t, lines, part * w + hi : part * w + w] = jnp.zeros((h, w - hi), jnp.bfloat16)

    def base(taps_ref):
        taps = taps_ref.shape[1]
        k = lax.broadcasted_iota(jnp.int32, (taps, 3 * h), 0)
        u = lax.broadcasted_iota(jnp.int32, (taps, 3 * h), 1)
        pick = (u == (taps - k if is_seed else k + 1)).astype(jnp.float32)
        return jnp.dot(
            taps_ref[...], pick, precision=lax.Precision.HIGHEST, preferred_element_type=jnp.float32
        )

    across_base, down_base = base(across_ref), base(down_ref)
    for t in range(terms):
        across_bands(t)
    arrived(has_down, to_up)
    for c, there in ((to_left[2], has_left), (to_right[2], has_right)):
        start(jnp.logical_and(has_down, there), c)
    arrived(has_up, to_down)
    for c, there in ((to_left[0], has_left), (to_right[0], has_right)):
        start(jnp.logical_and(has_up, there), c)
    w0, w1 = a + 2 * h, b + 2 * h

    def fill(e, source, at, width):
        head, rest = two_halves(pad[e, :, source : source + width])
        cols = slice(e * w1 + at, e * w1 + at + width)
        p_cat[0:w0, cols] = head
        p_cat[w0 : 2 * w0, cols] = rest
        p_cat[2 * w0 : 3 * w0, cols] = head

    def across(at, width):
        cols = slice(at, at + width)
        y_all[:, cols] = jnp.dot(a_cat[...], p_cat[:, cols], preferred_element_type=jnp.float32)

    for e in range(here):
        fill(e, h, 0, b)
        across(e * w1, b)
    for t in range(terms):
        down_bands(t)
    rows_of = (has_up, None, has_down)
    for k in range(3):
        for there, c in ((has_right, to_left[k]), (has_left, to_right[k])):
            arrived(there if k == 1 else jnp.logical_and(rows_of[k], there), c)
    for e in range(here):
        fill(e, 0, b, h)
        fill(e, h + b, b + h, h)
        across(e * w1 + b, 2 * h)
    acc[...] = jnp.zeros_like(acc)

    def weight(t, d, e):
        mine = die * here + e
        return mix_ref[t, mine * acc.shape[0] + d if is_seed else d * acc.shape[0] + mine]

    part = a // 2

    def along(half, t, carry):
        lines = pl.ds(pl.multiple_of(t * a + half * part, part), part)
        some = slice(half * part, (half + 1) * part)
        rows = jnp.concatenate(
            [
                jnp.concatenate(
                    [
                        y_all[lines, e * w1 + b : e * w1 + b + h],
                        y_all[lines, e * w1 : e * w1 + b],
                        y_all[lines, e * w1 + b + h : (e + 1) * w1],
                    ],
                    axis=1,
                )
                for e in range(here)
            ],
            axis=0,
        )
        head, rest = two_halves(rows)
        z = lax.dot_general(
            jnp.concatenate([head, head, rest], axis=1), d_cat[t],
            (((1,), (1,)), ((), ())), preferred_element_type=jnp.float32,
        )
        for d in range(acc.shape[0]):
            total = acc[d, some]
            for e in range(here):
                total = total + weight(t, d, e) * z[e * part : (e + 1) * part]
            acc[d, some] = total
        return carry

    shares = []
    for half in range(2):
        lax.fori_loop(0, terms, functools.partial(along, half), 0)
        some = pl.ds(half * part, part)
        share = copy(8 + half, acc.at[pl.ds((1 - die) * here, here), some], got.at[:, some], other)
        share.start()
        shares.append(share)
    for there, c in ((has_up, to_up), (has_down, to_down), (has_left, to_left[1]), (has_right, to_right[1])):
        ended(there, c)
    for k in (0, 2):
        for there, c in ((has_left, to_left[k]), (has_right, to_right[k])):
            ended(jnp.logical_and(rows_of[k], there), c)
    for share in shares:
        share.wait()
    out_ref[...] = acc[pl.ds(die * here, here)] + got[...]


def stage(fields, across_taps, down_taps, mix, is_seed):
    here, a, b = fields.shape
    terms, dies, _ = mix.shape
    w0, w1 = a + 2 * HALO, b + 2 * HALO
    vmem = pl.BlockSpec(memory_space=pltpu.VMEM)
    return pl.pallas_call(
        functools.partial(stage_kernel, is_seed),
        out_shape=jax.ShapeDtypeStruct(fields.shape, jnp.float32),
        in_specs=[vmem, vmem, vmem, pl.BlockSpec(memory_space=pltpu.SMEM)],
        out_specs=vmem,
        scratch_shapes=[
            pltpu.VMEM((here, w0, w1), jnp.float32),
            pltpu.VMEM((terms * a, 3 * w0), jnp.bfloat16),
            pltpu.VMEM((terms, b, 3 * w1), jnp.bfloat16),
            pltpu.VMEM((3 * w0, here * w1), jnp.bfloat16),
            pltpu.VMEM((terms * a, here * w1), jnp.float32),
            pltpu.VMEM((dies, a, b), jnp.float32),
            pltpu.VMEM((here, a, b), jnp.float32),
            pltpu.SemaphoreType.DMA((10,)),
            pltpu.SemaphoreType.DMA((10,)),
        ],
        compiler_params=pltpu.CompilerParams(
            collective_id=1 if is_seed else 0, has_side_effects=True, vmem_limit_bytes=48 * 2**20
        ),
    )(fields, across_taps, down_taps, mix.reshape(terms, dies * dies))


def swap_kernel(*refs):
    count = (len(refs) - 3) // 2
    sources, landed = refs[:count], refs[count : 2 * count]
    send, recv, keep = refs[2 * count :]
    across = lax.axis_size("col")
    peers = across * lax.axis_size("row")
    me = lax.axis_index("row") * across + lax.axis_index("col")
    barrier = pltpu.get_barrier_semaphore()

    def place(number):
        return {"row": number // across, "col": number % across}

    def greet(i, carry):
        pl.semaphore_signal(
            barrier, inc=1, device_id=place((me + i) % peers), device_id_type=pl.DeviceIdType.MESH
        )
        return carry

    def copies(i):
        to = (me + i) % peers
        return [
            pltpu.make_async_remote_copy(
                src_ref=src.at[:, to], dst_ref=dst.at[:, me],
                send_sem=send.at[k, i], recv_sem=recv.at[k, i],
                device_id=place(to), device_id_type=pl.DeviceIdType.MESH,
            )
            for k, (src, dst) in enumerate(zip(sources, landed))
        ]

    def begin(i, carry):
        for c in copies((i + peers // 2 - 2) % (peers - 1) + 1):
            c.start()
        return carry

    def finish(i, carry):
        for c in copies(i):
            c.wait()
        return carry

    lax.fori_loop(1, peers, greet, 0)
    pl.semaphore_wait(barrier, peers - 1)
    lax.fori_loop(1, peers, begin, 0)
    stay = [
        pltpu.make_async_copy(src.at[:, me], dst.at[:, me], keep.at[k])
        for k, (src, dst) in enumerate(zip(sources, landed))
    ]
    for c in stay:
        c.start()
    for c in stay:
        c.wait()
    lax.fori_loop(1, peers, finish, 0)


def swap(arrays, number):
    count, peers = len(arrays), arrays[0].shape[1]
    vmem = pl.BlockSpec(memory_space=pltpu.VMEM)
    return pl.pallas_call(
        swap_kernel,
        out_shape=[jax.ShapeDtypeStruct(x.shape, x.dtype) for x in arrays],
        in_specs=[vmem] * count,
        out_specs=[vmem] * count,
        scratch_shapes=[
            pltpu.SemaphoreType.DMA((count, peers)),
            pltpu.SemaphoreType.DMA((count, peers)),
            pltpu.SemaphoreType.DMA((count,)),
        ],
        compiler_params=pltpu.CompilerParams(
            collective_id=number, has_side_effects=True, vmem_limit_bytes=24 * 2**20
        ),
    )(*arrays)


def tiles_to_map(patch_totals_acc, tiles_down):
    dies_here, tile_total, cell_count = patch_totals_acc.shape
    mesh_layout = patch_totals_acc.reshape(
        dies_here, tile_total // tiles_down, tiles_down, PATCH_SIDE, PATCH_SIDE
    )
    return mesh_layout.transpose(0, 1, 3, 2, 4).reshape(
        dies_here, tile_total // tiles_down * PATCH_SIDE, tiles_down * PATCH_SIDE
    )


def map_to_tiles(source, tiles_down):
    dies_here, rows_all, cols_all = source.shape
    mesh_layout = source.reshape(
        dies_here, rows_all // PATCH_SIDE, PATCH_SIDE, tiles_down, PATCH_SIDE
    )
    return mesh_layout.transpose(0, 1, 3, 2, 4).reshape(dies_here, -1, PATCH_SIDE * PATCH_SIDE)


def local(parcel_patch, target_unit, target_patch, across_taps, down_taps, source_heated_mixing):
    dies_here, blocks_here, cells_tile = parcel_patch.shape
    devices_grid = lax.axis_size(("row", "col"))
    capacity = max(2, 2 * blocks_here // devices_grid)
    tiles_down = UNIT_MESH_Y // PATCH_SIDE
    destination = target_unit[:, :, 0]
    columns = jnp.arange(devices_grid, dtype=jnp.int32)
    same = destination[:, :, None] == destination[:, None, :]
    lines = jnp.arange(blocks_here, dtype=jnp.int32)
    earlier = lines[None, :] < lines[:, None]
    position = jnp.sum((same & earlier[None]).astype(jnp.int32), axis=2)
    slot_index = destination * capacity + position
    slots = jnp.arange(devices_grid * capacity, dtype=jnp.int32)
    place = (slot_index[:, :, None] == slots).astype(jnp.float32)
    outgoing = jnp.einsum("kbs,kbc->ksc", place, parcel_patch, precision=high)
    labels = jnp.sum(place * (target_patch.astype(jnp.float32) + 1.0)[:, :, None], axis=1) - 1.0
    span = dies_here * capacity
    rows = labels.reshape(dies_here, devices_grid, capacity).transpose(1, 0, 2).reshape(1, devices_grid, 1, span)
    rows = jnp.pad(rows, ((0, 0), (0, 0), (0, 0), (0, 128 - span)))
    arrived, arrived_rows = swap(
        (outgoing.reshape(dies_here, devices_grid, capacity, cells_tile), rows), 2
    )
    incoming = arrived.reshape(dies_here, -1, cells_tile)
    arrived_tile = arrived_rows[0, :, 0, :span].reshape(devices_grid, dies_here, capacity).transpose(1, 0, 2)
    target = arrived_tile.reshape(dies_here, -1).astype(jnp.int32)
    chosen = (target[:, :, None] == lines).astype(jnp.float32)
    patch_totals_acc = jnp.einsum("kst,ksc->ktc", chosen, incoming, precision=high)
    wattage_field = tiles_to_map(patch_totals_acc, tiles_down)
    chip_heat_increase = stage(wattage_field, across_taps, down_taps, source_heated_mixing, False)
    adjoint_field_map = stage(chip_heat_increase, across_taps, down_taps, source_heated_mixing, True)
    adjoint_patches = map_to_tiles(adjoint_field_map, tiles_down)
    answers = jnp.einsum("kst,ktc->ksc", chosen, adjoint_patches, precision=high)
    (returned,) = swap((answers.reshape(dies_here, devices_grid, capacity, cells_tile),), 3)
    block_power_slopes = jnp.einsum(
        "kbs,ksc->kbc", place, returned.reshape(dies_here, -1, cells_tile), precision=high
    )
    return (chip_heat_increase, block_power_slopes)


def solution(mesh):
    placed = (
        P("die", ("row", "col"), None),
        P("die", ("row", "col"), None),
        P("die", ("row", "col")),
        P(),
        P(),
        P(),
    )
    return jax.shard_map(
        local,
        mesh=mesh,
        in_specs=placed,
        out_specs=(P("die", "row", "col"), P("die", ("row", "col"), None)),
        check_vma=False,
    )
```
